32 devices in a mesh: dp: 8 (over y, x, core), tensor: 4 (over z).
Axes of the slice: x: 2, y: 2, z: 4, core: 2. Of those that a mesh axis runs over, the one named last changes fastest.
Arguments:
- hidden_in: bfloat16 [32768, 1024], P(('dp', 'tensor')), may hold values from -6 to 6
- segment_ids: int32 [8, 4096], P('dp'), may hold values from 0 to 3, never falling along the last dimension, each value on 1 to 3072 neighbouring positions
- norm_gain: bfloat16 [1024], P(('dp', 'tensor')), may hold values from 0.099609375 to 1.8984375
- w_zx: bfloat16 [1024, 2, 2048], P('dp', None, 'tensor'), may hold values from -0.1875 to 0.1875
- w_bc: bfloat16 [1024, 256], P(('dp', 'tensor')), may hold values from -0.1875 to 0.1875
- w_dt: bfloat16 [1024, 32], P('dp', 'tensor'), may hold values from -0.1875 to 0.1875
- conv_x: float32 [5, 2048], P(None, 'tensor'), may hold values from -3 to 3
- conv_bc: float32 [5, 256], replicated, may hold values from -3 to 3
- a_log: float32 [32], P('tensor'), may hold values from 0 to 2.77
- dt_bias: float32 [32], P('tensor'), may hold values from -6.9 to -2.25
- skip_gain: float32 [32], P('tensor'), may hold values from 0.5 to 1.5
- gnorm_gain: bfloat16 [2048], P('tensor'), may hold values from 0.099609375 to 1.8984375
- w_out: bfloat16 [1024, 2048], P('dp', 'tensor'), may hold values from -0.125 to 0.125
- grad_out: bfloat16 [32768, 1024], P(('dp', 'tensor')), may hold values from -6 to 6
Outputs:
- mixed: bfloat16 [32768, 1024], P(('dp', 'tensor'))
- grad_input: float32 [32768, 1024], P(('dp', 'tensor'))
- grad_norm_gain: float32 [1024], P(('dp', 'tensor'))
- grad_w_zx: float32 [1024, 2, 2048], P('dp', None, 'tensor')
- grad_w_bc: float32 [1024, 256], P(('dp', 'tensor'))
- grad_w_dt: float32 [1024, 32], P('dp', 'tensor')
- grad_conv_x: float32 [5, 2048], P(None, 'tensor')
- grad_conv_bc: float32 [5, 256], replicated
- grad_a_log: float32 [32], P('tensor')
- grad_dt_bias: float32 [32], P('tensor')
- grad_skip_gain: float32 [32], P('tensor')
- grad_gnorm_gain: float32 [2048], P('tensor')
- grad_w_out: float32 [1024, 2048], P('dp', 'tensor')
The draws below stay inside these ranges and needn't reach their ends.
Inputs may be any that keep to these rules, and one draw needn't show every extreme that they name: `segment_ids`: in each sequence the numbers never fall and start at 0; each document has at most 3072 positions, and one has exactly that many.
All inputs are finite; a program needn't handle non-finite values.
Results may differ from the reference program's by a relative error of at most 0.017.
Values may be sent and summed in bfloat16 or wider, within the bound.
A program may use at most 256 MiB of HBM per device.

```python
import math
import jax
import jax.numpy as jnp
import numpy as np
from jax import lax

D = 1024
HEADS = 32
STATE = 128
CONV = 4
BLOCK_LEN = 256
INNER = 2048
SEQ_LEN = 4096
SEQS = 8
TOKENS = 32768


def block_levels(key, extent, split, smallest, largest):
    def one(axis_at, parts):
        draws = jax.random.uniform(jax.random.fold_in(jax.random.fold_in(key, 6), axis_at), (parts,), jnp.float32, smallest / len(split), largest / len(split))
        return jnp.repeat(jnp.exp(draws), extent[axis_at] // parts).reshape((-1,) + (1,) * (len(extent) - axis_at - 1))

    loudness = one(*split[0])
    for cut in split[1:]:
        loudness = loudness * one(*cut)
    return loudness


def length_profile(amount, total, most, lean):
    weights = [(1 << 20) // math.isqrt(rank ** lean) + 1 for rank in range(2, amount + 1)]
    rest, given = total - most - (amount - 1), [1] * (amount - 1)
    while rest > 0:
        movable = [i for i in range(amount - 1) if given[i] < most]
        pool, left = sum([weights[i] for i in movable]), rest
        for i in movable:
            more = min(most - given[i], max(1, left * weights[i] // pool), rest)
            given[i] = given[i] + more
            rest = rest - more
    return np.array([most] + given)


def ragged(own_key, amount, total, limit, lean):
    if amount == 2:
        one = jax.random.randint(own_key, (), max(1, total - limit), min(limit, total - 1) + 1)
        return jnp.stack([one, total - one])
    sizes = jnp.asarray(length_profile(amount, total, limit, lean), jnp.int32)
    couples = (amount - 1) // 2
    donor, receiver = sizes[1:1 + 2 * couples:2], sizes[2:2 + 2 * couples:2]
    margin = jnp.minimum(donor - 1, limit - receiver)
    moved = jax.random.randint(jax.random.fold_in(own_key, 1), (couples,), 0, 1 << 20) % (margin + 1)
    sizes = sizes.at[1:1 + 2 * couples:2].set(donor - moved).at[2:2 + 2 * couples:2].set(receiver + moved)
    return sizes[jax.random.permutation(jax.random.fold_in(own_key, 2), amount)]


def scatter_about(own_key, dims, scale, limit, cuts=(), kind=jnp.bfloat16):
    gain = block_levels(own_key, dims, cuts, -0.22, 0.18) if cuts else 1.0
    values = jax.random.normal(own_key, dims, jnp.float32) * scale * gain
    return jnp.minimum(jnp.maximum(values, -limit), limit).astype(kind)


def setup_inputs(seed: int = 0) -> dict:
    arg_keys = jax.random.split(jax.random.key(seed), 15)
    hidden_in = scatter_about(arg_keys[0], (TOKENS, D), 1.0, 6.0, ((0, 32),))
    segment_ids = jax.vmap(lambda own: jnp.searchsorted(jnp.cumsum(ragged(own, 4, SEQ_LEN, 3 * SEQ_LEN // 4, 0)), jnp.arange(SEQ_LEN), side="right"))(jax.random.split(arg_keys[1], SEQS)).reshape((SEQS, SEQ_LEN)).astype(jnp.int32)
    norm_gain = jnp.clip(1.0 + 0.18 * jax.random.normal(arg_keys[2], (D,), jnp.float32), 0.099609375, 1.8984375).astype(jnp.bfloat16)
    w_zx = scatter_about(arg_keys[3], (D, 2, INNER), D ** -0.5, 0.1875, ((0, 8), (2, 4)))
    w_bc = scatter_about(arg_keys[4], (D, 2 * STATE), D ** -0.5, 0.1875, ((0, 32),))
    w_dt = scatter_about(arg_keys[5], (D, HEADS), D ** -0.5, 0.1875, ((0, 8), (1, 4)))
    conv_x = scatter_about(arg_keys[6], (CONV + 1, INNER), 0.5, 3.0, ((1, 4),), jnp.float32)
    conv_bc = scatter_about(arg_keys[7], (CONV + 1, 2 * STATE), 0.5, 3.0, (), jnp.float32)
    a_log = jnp.clip(2.77 * jax.random.uniform(arg_keys[8], (HEADS,), jnp.float32) ** block_levels(arg_keys[8], (HEADS,), ((0, 4),), -0.2, 0.2), 0.0, 2.77)
    dt_bias = jnp.clip(-6.9 + 4.65 * jax.random.uniform(arg_keys[9], (HEADS,), jnp.float32) ** block_levels(arg_keys[9], (HEADS,), ((0, 4),), -0.2, 0.2), -6.9, -2.25)
    skip_gain = jnp.clip(0.5 + 1.0 * jax.random.uniform(arg_keys[10], (HEADS,), jnp.float32) ** block_levels(arg_keys[10], (HEADS,), ((0, 4),), -0.2, 0.2), 0.5, 1.5)
    gnorm_gain = jnp.clip(1.0 + 0.18 * jax.random.normal(arg_keys[11], (INNER,), jnp.float32), 0.099609375, 1.8984375).astype(jnp.bfloat16)
    w_out = scatter_about(arg_keys[12], (D, INNER), INNER ** -0.5, 0.125, ((0, 8), (1, 4)))
    grad_out = scatter_about(arg_keys[13], (TOKENS, D), 1.0, 6.0, ((0, 32),))
    return dict(hidden_in=hidden_in, segment_ids=segment_ids, norm_gain=norm_gain, w_zx=w_zx, w_bc=w_bc, w_dt=w_dt, conv_x=conv_x, conv_bc=conv_bc, a_log=a_log, dt_bias=dt_bias, skip_gain=skip_gain, gnorm_gain=gnorm_gain, w_out=w_out, grad_out=grad_out)


@jax.custom_vjp
def low(v):
    return lax.optimization_barrier(v.astype(jnp.bfloat16)).astype(jnp.float32)

@jax.custom_vjp
def low_back(v):
    return v

def low_keep(v):
    return (low(v), None)

def low_pass(kept, grad):
    return (grad,)

def back_keep(v):
    return (v, None)

def back_low(kept, grad):
    return (low(grad),)
low.defvjp(low_keep, low_pass)
low_back.defvjp(back_keep, back_low)
epsilon = 1e-05
exact_mode = lax.Precision.HIGHEST

def causal_conv(values, weights, segments):
    taps = weights.shape[0] - 1
    length = values.shape[0]
    padded = jnp.concatenate([jnp.zeros((taps - 1, values.shape[1]), values.dtype), values], axis=0)
    seg_pad = jnp.concatenate([jnp.full((taps - 1,), -1, jnp.int32), segments.astype(jnp.int32)])
    summed = jnp.zeros_like(values) + weights[taps]
    for offset in range(taps):
        matched = seg_pad[offset:offset + length] == segments.astype(jnp.int32)
        summed = summed + weights[offset] * jnp.where(matched[:, None], padded[offset:offset + length], 0.0)
    return summed

def block_step(running, pieces):
    carry_state, before = running
    x_blk, b_blk, c_blk, a_blk, dt_blk, s_blk = pieces
    span_len = s_blk.shape[0]
    cumulative = jnp.cumsum(a_blk, axis=0).T
    row_ids = lax.broadcasted_iota(jnp.int32, (span_len, span_len), 0)
    col_ids = lax.broadcasted_iota(jnp.int32, (span_len, span_len), 1)
    allowed = (s_blk[:, None] == s_blk[None, :]) & (row_ids >= col_ids)
    gaps = cumulative[:, :, None] - cumulative[:, None, :]
    decays = jnp.exp(jnp.where(allowed[None], gaps, -jnp.inf))
    inner_prod = jnp.dot(c_blk, b_blk.T, precision=exact_mode)
    scores = inner_prod[None] * decays * dt_blk.T[:, None, :]
    y_local = jnp.einsum('hij,jhp->ihp', scores, x_blk, precision=exact_mode)
    start_w = jnp.where((s_blk == before)[:, None], jnp.exp(cumulative.T), 0.0)
    y_carry = jnp.einsum('in,hpn->ihp', c_blk, carry_state, precision=exact_mode) * start_w[:, :, None]
    last_seg = s_blk[span_len - 1]
    tail_weight = jnp.where((s_blk == last_seg)[:, None], jnp.exp(cumulative[:, span_len - 1:] - cumulative).T, 0.0) * dt_blk
    kept_share = jnp.where(last_seg == before, jnp.exp(cumulative[:, span_len - 1]), 0.0)
    new_state = jnp.einsum('jh,jhp,jn->hpn', tail_weight, x_blk, b_blk, precision=exact_mode)
    new_state = new_state + kept_share[:, None, None] * carry_state
    return ((new_state, last_seg), y_local + y_carry)

def scan_mix(inputs_x, in_map, out_map, step_size, rates, segments, block_len):
    length, head_count = step_size.shape
    blocks = length // block_len
    x_blocks = inputs_x.reshape(blocks, block_len, head_count, -1)
    a_blocks = (step_size * rates).reshape(blocks, block_len, head_count)
    start_state = jnp.zeros((head_count, x_blocks.shape[3], in_map.shape[1]), inputs_x.dtype)
    pieces = (x_blocks, in_map.reshape(blocks, block_len, -1), out_map.reshape(blocks, block_len, -1), a_blocks, step_size.reshape(blocks, block_len, head_count), segments.astype(jnp.int32).reshape(blocks, block_len))
    ending, outputs = lax.scan(jax.checkpoint(block_step), (start_state, jnp.array(-1, jnp.int32)), pieces)
    return outputs.reshape(length, -1)

def ssm_mixer(inner_x, bc_raw, dt_raw, conv_x, conv_bc, a_log, dt_bias, skip_gain, segments, block_len):
    inputs_x = jax.nn.silu(causal_conv(inner_x, conv_x, segments))
    state_maps = jax.nn.silu(causal_conv(bc_raw, conv_bc, segments))
    half_cols = state_maps.shape[1] // 2
    step_size = jax.nn.softplus(dt_raw + dt_bias)
    head_count = step_size.shape[1]
    scanned = scan_mix(inputs_x, state_maps[:, :half_cols], state_maps[:, half_cols:], step_size, -jnp.exp(a_log), segments, block_len)
    direct = (inputs_x.reshape(inputs_x.shape[0], head_count, -1) * skip_gain[:, None]).reshape(inputs_x.shape)
    return scanned + direct

def one_sequence(hidden, segments, params):
    norm_gain, w_zx, w_bc, w_dt, conv_x, conv_bc, a_log, dt_bias, skip_gain, gnorm_gain, w_out = params
    normed = low(hidden * lax.rsqrt(lax.optimization_barrier(jnp.mean(hidden * hidden, -1, keepdims=True)) + epsilon) * norm_gain)
    gate_z = low(low_back(jnp.dot(normed, w_zx[:, 0], precision=exact_mode)))
    inner_x = low_back(jnp.dot(normed, w_zx[:, 1], precision=exact_mode))
    bc_raw = low_back(jnp.dot(normed, w_bc, precision=exact_mode))
    dt_raw = low_back(jnp.dot(normed, w_dt, precision=exact_mode))
    mixed_y = low(low_back(ssm_mixer(inner_x, bc_raw, dt_raw, conv_x, conv_bc, a_log, dt_bias, skip_gain, segments, BLOCK_LEN)))
    gated = mixed_y * jax.nn.silu(gate_z)
    normed_gate = low(gated * lax.rsqrt(lax.optimization_barrier(jnp.mean(gated * gated, -1, keepdims=True)) + epsilon) * gnorm_gain)
    return hidden + jnp.dot(normed_gate, w_out.T, precision=exact_mode)

def reference(hidden_in, segment_ids, norm_gain, w_zx, w_bc, w_dt, conv_x, conv_bc, a_log, dt_bias, skip_gain, gnorm_gain, w_out, grad_out):
    params = tuple((p.astype(jnp.float32) for p in (norm_gain, w_zx, w_bc, w_dt, conv_x, conv_bc, a_log, dt_bias, skip_gain, gnorm_gain, w_out)))
    hidden = hidden_in.astype(jnp.float32).reshape(SEQS, SEQ_LEN, D)

    def forward(hidden_all, param_set):

        def per_sequence(packed):
            return jax.checkpoint(one_sequence)(packed[0], packed[1], param_set)
        return lax.map(per_sequence, (hidden_all, segment_ids))
    result, backward = jax.vjp(forward, hidden, params)
    d_hidden, d_params = backward(grad_out.astype(jnp.float32).reshape(SEQS, SEQ_LEN, D))
    return (result.reshape(TOKENS, D).astype(jnp.bfloat16), d_hidden.reshape(TOKENS, D), d_params[0], d_params[1], d_params[2], d_params[3], d_params[4], d_params[5], d_params[6], d_params[7], d_params[8], d_params[9], d_params[10])
```

```python
import jax
import jax.numpy as jnp
from jax import lax
from jax.experimental import pallas as pl
from jax.experimental.pallas import tpu as pltpu
from jax.sharding import PartitionSpec as P

BLOCK_LEN = 256


epsilon = 1e-05
exact_mode = lax.Precision.HIGHEST


def causal_conv(values, weights, segments):
    taps = weights.shape[0] - 1
    length = values.shape[0]
    padded = jnp.concatenate([jnp.zeros((taps - 1, values.shape[1]), values.dtype), values], axis=0)
    seg_pad = jnp.concatenate([jnp.full((taps - 1,), -1, jnp.int32), segments])
    summed = jnp.zeros_like(values) + weights[taps]
    for offset in range(taps):
        matched = seg_pad[offset : offset + length] == segments
        summed = summed + weights[offset] * jnp.where(
            matched[:, None], padded[offset : offset + length], 0.0
        )
    return summed


def exact_dot(left, right, dims):
    return lax.dot_general(
        left, right, (dims, ((), ())), precision=exact_mode, preferred_element_type=jnp.float32
    )


def low_dot(left, right, dims):
    return lax.dot_general(
        left.astype(jnp.bfloat16),
        right.astype(jnp.bfloat16),
        (dims, ((), ())),
        preferred_element_type=jnp.float32,
    )


ROWS_COLS = ((1,), (0,))
COLS_COLS = ((1,), (1,))
ROWS_ROWS = ((0,), (0,))


def block_terms(x_ref, bc_ref, cols_ref, rows_ref, rate_row_ref, rate_col_ref):
    heads = rate_row_ref.shape[1]
    span, inner = x_ref.shape
    width = inner // heads
    half = bc_ref.shape[1] // 2
    cols = cols_ref[...]
    rows = rows_ref[...]
    dt = cols[:, :heads]
    start = cols[:, heads + 1 : heads + 2]
    tail = cols[:, heads + 2 : heads + 3]
    row_ids = lax.broadcasted_iota(jnp.int32, (span, span), 0)
    col_ids = lax.broadcasted_iota(jnp.int32, (span, span), 1)
    lower = row_ids >= col_ids
    tri = jnp.where(lower, 1.0, 0.0)
    allowed = lower & (cols[:, heads : heads + 1] == rows[heads : heads + 1, :])
    cum_col = exact_dot(tri, dt * rate_row_ref[...], ROWS_COLS)
    cum_row = exact_dot(rows[:heads, :] * rate_col_ref[...], tri, COLS_COLS)
    total = cum_col[span - 1 : span, :]
    last_start = start[span - 1 : span, :]
    kept = last_start * jnp.exp(total)
    head_ids = lax.broadcasted_iota(jnp.int32, (heads, inner), 0)
    chan_ids = lax.broadcasted_iota(jnp.int32, (heads, inner), 1)
    member = jnp.where(
        (chan_ids >= head_ids * width) & (chan_ids < (head_ids + 1) * width), 1.0, 0.0
    )
    spread = exact_dot(
        jnp.concatenate([dt, start * jnp.exp(cum_col), tail * jnp.exp(total - cum_col)], axis=0),
        member,
        ROWS_COLS,
    )
    kept_wide = jnp.broadcast_to(
        last_start * jnp.exp(cum_row[:, span - 1 : span]), (heads, half)
    )
    kept_state = exact_dot(member, kept_wide, ROWS_ROWS)
    x = x_ref[...]
    dt_wide, start_wide, tail_wide = spread[:span], spread[span : 2 * span], spread[2 * span :]
    in_map = bc_ref[:, :half].astype(jnp.bfloat16)
    out_map = bc_ref[:, half:].astype(jnp.bfloat16)
    inner_prod = low_dot(out_map, in_map, COLS_COLS)

    def decay(head):
        gaps = cum_col[:, head : head + 1] - cum_row[head : head + 1, :]
        return jnp.exp(jnp.where(allowed, gaps, -jnp.inf))

    return (
        heads, width, x, x * dt_wide, dt_wide, start_wide, tail_wide,
        in_map, out_map, inner_prod, decay, kept, kept_state, member, tri,
    )


def forward_kernel(
    x_ref, bc_ref, cols_ref, rows_ref, rate_row_ref, rate_col_ref, skip_ref,
    y_ref, states_ref, state,
):
    @pl.when(pl.program_id(0) == 0)
    def _():
        state[...] = jnp.zeros_like(state)

    (heads, width, x, x_dt, dt_wide, start_wide, tail_wide,
     in_map, out_map, inner_prod, decay, kept, kept_state, member, tri) = block_terms(
        x_ref, bc_ref, cols_ref, rows_ref, rate_row_ref, rate_col_ref
    )
    before = state[...]
    states_ref[0] = before
    x_low = x_dt.astype(jnp.bfloat16)
    local = [
        low_dot(inner_prod * decay(h), x_low[:, h * width : (h + 1) * width], ROWS_COLS)
        for h in range(heads)
    ]
    y = jnp.concatenate(local, axis=1) + start_wide * low_dot(out_map, before, COLS_COLS)
    y_ref[...] = (y + skip_ref[...] * x).astype(y_ref.dtype)
    state[...] = kept_state * before + low_dot(x_dt * tail_wide, in_map, ROWS_ROWS)


def backward_kernel(
    x_ref, bc_ref, cols_ref, rows_ref, rate_row_ref, rate_col_ref, skip_ref, dy_ref, states_ref,
    dx_ref, dbc_ref, ddt_ref, da_ref, dskip_ref, dstate,
):
    @pl.when(pl.program_id(0) == 0)
    def _():
        dstate[...] = jnp.zeros_like(dstate)
        dskip_ref[...] = jnp.zeros_like(dskip_ref)

    (heads, width, x, x_dt, dt_wide, start_wide, tail_wide,
     in_map, out_map, inner_prod, decay, kept, kept_state, member, tri) = block_terms(
        x_ref, bc_ref, cols_ref, rows_ref, rate_row_ref, rate_col_ref
    )
    half = in_map.shape[1]
    before = states_ref[0]
    after_grad = dstate[...]
    dy_low = dy_ref[...]
    dy = dy_low.astype(jnp.float32)
    x_low = x_dt.astype(jnp.bfloat16)
    local, back = [], []
    d_prod = jnp.zeros_like(inner_prod)
    for h in range(heads):
        part = slice(h * width, (h + 1) * width)
        fade = decay(h)
        scores = (inner_prod * fade).astype(jnp.bfloat16)
        local.append(low_dot(scores, x_low[:, part], ROWS_COLS))
        back.append(low_dot(scores, dy_low[:, part], ROWS_ROWS))
        d_prod = d_prod + low_dot(dy_low[:, part], x_low[:, part], COLS_COLS) * fade
    dy_start = (dy * start_wide).astype(jnp.bfloat16)
    x_tail = (x_dt * tail_wide).astype(jnp.bfloat16)
    y = jnp.concatenate(local, axis=1) + start_wide * low_dot(out_map, before, COLS_COLS)
    from_state = tail_wide * low_dot(in_map, after_grad, COLS_COLS)
    local_back = jnp.concatenate(back, axis=1)
    d_xdt = local_back + from_state
    x_exact = x_low.astype(jnp.float32)
    tail_terms = from_state * x_exact
    d_cum_wide = dy * y - local_back * x_exact - tail_terms
    d_both = exact_dot(
        jnp.concatenate([d_cum_wide, d_xdt * x], axis=0), member, COLS_COLS
    )
    span = x.shape[0]
    tail_sum = jnp.sum(tail_terms, axis=0, keepdims=True)
    kept_sum = exact_dot(jnp.ones((8, half), jnp.float32), after_grad * before, COLS_COLS)
    last_both = exact_dot(
        jnp.concatenate([jnp.broadcast_to(tail_sum, kept_sum.shape), kept_sum], axis=0),
        member,
        COLS_COLS,
    )
    d_last = last_both[0:1] + kept * last_both[8:9]
    d_a = exact_dot(tri, d_both[:span], ROWS_ROWS) + d_last
    da_ref[...] = d_a
    ddt_ref[...] = d_both[span:] + d_a * rate_row_ref[...]
    dx_ref[...] = d_xdt * dt_wide + skip_ref[...] * dy
    dskip_ref[...] += jnp.broadcast_to(jnp.sum(dy * x, axis=0, keepdims=True), dskip_ref.shape)
    dbc_ref[:, :half] = low_dot(d_prod, out_map, ROWS_ROWS) + low_dot(
        x_tail, after_grad, ROWS_COLS
    )
    dbc_ref[:, half:] = low_dot(d_prod, in_map, ROWS_COLS) + low_dot(dy_start, before, ROWS_COLS)
    dstate[...] = kept_state * after_grad + low_dot(dy_start, out_map, ROWS_ROWS)


def block_specs(length, inner, maps, lanes, heads, order):
    return [
        pl.BlockSpec((BLOCK_LEN, inner), lambda i: (order(i), 0)),
        pl.BlockSpec((BLOCK_LEN, maps), lambda i: (order(i), 0)),
        pl.BlockSpec((BLOCK_LEN, lanes), lambda i: (order(i), 0)),
        pl.BlockSpec((lanes, BLOCK_LEN), lambda i: (0, order(i))),
        pl.BlockSpec((1, heads), lambda i: (0, 0)),
        pl.BlockSpec((heads, 1), lambda i: (0, 0)),
        pl.BlockSpec((1, inner), lambda i: (0, 0)),
    ]


def limits():
    return pltpu.CompilerParams(vmem_limit_bytes=48 * 1024 * 1024)


def scan_forward(xs, maps, cols, rows, rates, skip_wide):
    length, inner = xs.shape
    heads = rates.shape[0]
    half = maps.shape[1] // 2
    blocks = length // BLOCK_LEN
    return pl.pallas_call(
        forward_kernel,
        grid=(blocks,),
        in_specs=block_specs(length, inner, maps.shape[1], cols.shape[1], heads, lambda i: i),
        out_specs=[
            pl.BlockSpec((BLOCK_LEN, inner), lambda i: (i, 0)),
            pl.BlockSpec((1, inner, half), lambda i: (i, 0, 0)),
        ],
        out_shape=[
            jax.ShapeDtypeStruct((length, inner), jnp.bfloat16),
            jax.ShapeDtypeStruct((blocks, inner, half), jnp.float32),
        ],
        scratch_shapes=[pltpu.VMEM((inner, half), jnp.float32)],
        compiler_params=limits(),
        cost_estimate=pl.CostEstimate(
            flops=12 * 10**9, bytes_accessed=24 * 10**6, transcendentals=10**7
        ),
        name="scan_forward",
    )(xs, maps, cols, rows, rates[None, :], rates[:, None], skip_wide)


def scan_backward(xs, maps, cols, rows, rates, skip_wide, dy, states):
    length, inner = xs.shape
    heads = rates.shape[0]
    half = maps.shape[1] // 2
    blocks = length // BLOCK_LEN
    last = blocks - 1
    return pl.pallas_call(
        backward_kernel,
        grid=(blocks,),
        in_specs=block_specs(
            length, inner, maps.shape[1], cols.shape[1], heads, lambda i: last - i
        )
        + [
            pl.BlockSpec((BLOCK_LEN, inner), lambda i: (last - i, 0)),
            pl.BlockSpec((1, inner, half), lambda i: (last - i, 0, 0)),
        ],
        out_specs=[
            pl.BlockSpec((BLOCK_LEN, inner), lambda i: (last - i, 0)),
            pl.BlockSpec((BLOCK_LEN, 2 * half), lambda i: (last - i, 0)),
            pl.BlockSpec((BLOCK_LEN, heads), lambda i: (last - i, 0)),
            pl.BlockSpec((BLOCK_LEN, heads), lambda i: (last - i, 0)),
            pl.BlockSpec((8, inner), lambda i: (0, 0)),
        ],
        out_shape=[
            jax.ShapeDtypeStruct((length, inner), jnp.float32),
            jax.ShapeDtypeStruct((length, 2 * half), jnp.float32),
            jax.ShapeDtypeStruct((length, heads), jnp.float32),
            jax.ShapeDtypeStruct((length, heads), jnp.float32),
            jax.ShapeDtypeStruct((8, inner), jnp.float32),
        ],
        scratch_shapes=[pltpu.VMEM((inner, half), jnp.float32)],
        compiler_params=limits(),
        cost_estimate=pl.CostEstimate(
            flops=30 * 10**9, bytes_accessed=40 * 10**6, transcendentals=10**7
        ),
        name="scan_backward",
    )(xs, maps, cols, rows, rates[None, :], rates[:, None], skip_wide, dy, states)


def scan_inputs(step, segments):
    length, heads = step.shape
    ends = segments.reshape(-1, BLOCK_LEN)[:, -1]
    before = jnp.concatenate([jnp.full((1,), -1, segments.dtype), ends[:-1]])
    blocked = segments.reshape(-1, BLOCK_LEN)
    start = (blocked == before[:, None]).reshape(-1)
    tail = (blocked == ends[:, None]).reshape(-1)
    marks = jnp.stack([segments, start, tail], axis=0).astype(jnp.float32)
    extra = -(heads + 3) % 8
    rows = jnp.concatenate([step.T, marks, jnp.zeros((extra, length), jnp.float32)], axis=0)
    return rows.T, rows


def conv_parts(inner_x, bc_raw, dt_raw, conv_x, conv_bc, dt_bias, segments):
    xs = jax.nn.silu(causal_conv(inner_x, conv_x, segments))
    maps = jax.nn.silu(causal_conv(bc_raw, conv_bc, segments))
    return xs, maps, jax.nn.softplus(dt_raw + dt_bias)


def contract_rows(left, right):
    return lax.dot_general(
        left, right, (((0,), (0,)), ((), ())), preferred_element_type=jnp.float32
    )


def contract_cols(left, right):
    return lax.dot_general(
        left, right, (((1,), (1,)), ((), ())), preferred_element_type=jnp.float32
    )


def spread_part(part, axis_pos, parts, rank):
    full_shape = list(part.shape)
    full_shape[axis_pos] = part.shape[axis_pos] * parts
    zeros_full = jnp.zeros(tuple(full_shape), jnp.float32)
    return lax.dynamic_update_slice_in_dim(zeros_full, part, rank * part.shape[axis_pos], axis_pos)


def body(
    hidden_in,
    segment_ids,
    norm_gain,
    w_zx,
    w_bc,
    w_dt,
    conv_x,
    conv_bc,
    a_log,
    dt_bias,
    skip_gain,
    gnorm_gain,
    w_out,
    grad_out,
):
    model_dim = hidden_in.shape[1]
    tensor_count = lax.axis_size("tensor")
    tensor_rank = lax.axis_index("tensor")
    rows_loc = w_zx.shape[0]
    inner_loc = w_zx.shape[2]
    heads = w_dt.shape[1]
    maps_dim = w_bc.shape[1]
    inner_total = inner_loc * tensor_count
    hidden_all = lax.all_gather(hidden_in, "tensor", axis=0, tiled=True)
    few = jnp.concatenate([w_bc, jnp.pad(norm_gain[:, None], ((0, 0), (0, 127)))], axis=1)
    few_rows = lax.all_gather(few, "tensor", axis=0, tiled=True)
    w_mine = jnp.concatenate(
        [
            w_zx.reshape(rows_loc, 2 * inner_loc),
            few_rows[:, :maps_dim],
            w_dt,
            few_rows[:, maps_dim : maps_dim + 128 - heads],
        ],
        axis=1,
    )
    w_all = lax.all_gather(w_mine, "dp", axis=0, tiled=True)
    w_out_rows = lax.all_gather(w_out, "dp", axis=0, tiled=True)
    cot_all = lax.all_gather(grad_out, "tensor", axis=0, tiled=True)
    bc_at = 2 * inner_loc
    dt_at = bc_at + maps_dim
    gain_val = w_all[:, dt_at + heads].astype(jnp.float32)
    hidden = hidden_in.astype(jnp.float32)
    pre_scale = lax.rsqrt(jnp.mean(hidden * hidden, -1, keepdims=True) + epsilon)
    hidden_val = hidden_all.astype(jnp.float32)
    scale_all = lax.rsqrt(jnp.mean(hidden_val * hidden_val, -1, keepdims=True) + epsilon)
    normed_all = (hidden_val * scale_all * gain_val).astype(jnp.bfloat16)
    gate_low = jnp.dot(
        normed_all, w_all[:, :inner_loc], preferred_element_type=jnp.float32
    ).astype(jnp.bfloat16)
    inner_x = jnp.dot(
        normed_all, w_all[:, inner_loc:bc_at], preferred_element_type=jnp.float32
    )
    few_proj = jnp.dot(normed_all, w_all[:, bc_at:], preferred_element_type=jnp.float32)
    bc_raw = few_proj[:, :maps_dim]
    dt_raw = few_proj[:, maps_dim : maps_dim + heads]
    segments = segment_ids[0]

    def local_conv(inner_in, bc_in, dt_in, conv_xin, conv_bcin, dt_biasin):
        return conv_parts(inner_in, bc_in, dt_in, conv_xin, conv_bcin, dt_biasin, segments)

    (xs, maps, step), conv_back = jax.vjp(
        local_conv, inner_x, bc_raw, dt_raw, conv_x, conv_bc, dt_bias
    )
    rates = -jnp.exp(a_log)
    width = inner_loc // heads
    skip_wide = jnp.repeat(skip_gain, width)[None, :]
    cols, rows = scan_inputs(step, segments)
    y_low, states = scan_forward(xs, maps, cols, rows, rates, skip_wide)
    y_val = y_low.astype(jnp.float32)
    z_val = gate_low.astype(jnp.float32)
    sigma_z = jax.nn.sigmoid(z_val)
    gated = y_val * z_val * sigma_z
    gn_gain = gnorm_gain.astype(jnp.float32)
    d_gate_norm = jnp.dot(cot_all, w_out_rows, preferred_element_type=jnp.float32)
    scaled_grad = d_gate_norm * gn_gain
    token_sums = lax.psum(
        jnp.stack([jnp.sum(gated * gated, -1), jnp.sum(scaled_grad * gated, -1)]), "tensor"
    )
    gate_scale = lax.rsqrt(token_sums[0] / inner_total + epsilon)[:, None]
    cross_sum = token_sums[1]
    d_gated = gate_scale * scaled_grad - gated * gate_scale**3 * (cross_sum / inner_total)[:, None]
    dy_low = (d_gated * z_val * sigma_z).astype(jnp.bfloat16)
    dz_low = (d_gated * y_val * sigma_z * (1.0 + z_val * (1.0 - sigma_z))).astype(jnp.bfloat16)
    normed_gate = (gated * gate_scale * gn_gain).astype(jnp.bfloat16)
    d_gain_part = jnp.sum(d_gate_norm * gated * gate_scale, 0)
    branch = lax.psum_scatter(
        contract_cols(normed_gate, w_out_rows).astype(jnp.bfloat16),
        "tensor",
        scatter_dimension=0,
        tiled=True,
    ).astype(jnp.float32)
    mixed = (hidden + branch).astype(jnp.bfloat16)
    g_out = lax.psum_scatter(
        contract_rows(cot_all, normed_gate).astype(jnp.bfloat16),
        "dp",
        scatter_dimension=0,
        tiled=True,
    ).astype(jnp.float32)
    dxs, dmaps, dstep, d_rate_terms, dskip_rows = scan_backward(
        xs, maps, cols, rows, rates, skip_wide, dy_low, states
    )
    d_a_log = jnp.sum(d_rate_terms * step, 0) * rates
    d_skip = jnp.sum(dskip_rows[0].reshape(heads, width), 1)
    d_inner, d_bc, d_dt, d_conv_x, d_conv_bc, d_dt_bias = conv_back((dxs, dmaps, dstep))
    d_all = jnp.concatenate(
        [
            dz_low,
            d_inner.astype(jnp.bfloat16),
            d_bc.astype(jnp.bfloat16),
            d_dt.astype(jnp.bfloat16),
            jnp.zeros((d_dt.shape[0], 128 - heads), jnp.bfloat16),
        ],
        axis=1,
    )
    term = contract_cols(d_all, w_all).astype(jnp.bfloat16)
    d_normed = lax.psum_scatter(term, "tensor", scatter_dimension=0, tiled=True).astype(
        jnp.float32
    )
    d_w = contract_rows(normed_all, d_all).astype(jnp.bfloat16)
    g_all = lax.psum_scatter(d_w, "dp", scatter_dimension=0, tiled=True)
    g_bc = lax.psum_scatter(
        g_all[:, bc_at:dt_at], "tensor", scatter_dimension=0, tiled=True
    ).astype(jnp.float32)
    g_zx = g_all[:, :bc_at].astype(jnp.float32).reshape(rows_loc, 2, inner_loc)
    g_dt = g_all[:, dt_at : dt_at + heads].astype(jnp.float32)
    pre_grad = d_normed * gain_val
    d_hidden = pre_scale * pre_grad - hidden * pre_scale**3 * jnp.mean(
        pre_grad * hidden, -1, keepdims=True
    )
    grad_input = grad_out.astype(jnp.float32) + d_hidden
    d_norm_gain = jnp.sum(d_normed * hidden * pre_scale, 0)
    sums_all = lax.psum(
        (
            spread_part(d_conv_x, 1, tensor_count, tensor_rank),
            d_conv_bc,
            spread_part(d_a_log, 0, tensor_count, tensor_rank),
            spread_part(d_dt_bias, 0, tensor_count, tensor_rank),
            spread_part(d_skip, 0, tensor_count, tensor_rank),
            spread_part(d_gain_part, 0, tensor_count, tensor_rank),
            d_norm_gain,
        ),
        ("dp", "tensor"),
    )
    head_loc = d_a_log.shape[0]
    g_conv_x = lax.dynamic_slice_in_dim(sums_all[0], tensor_rank * inner_loc, inner_loc, 1)
    g_a_log = lax.dynamic_slice_in_dim(sums_all[2], tensor_rank * head_loc, head_loc, 0)
    g_dt_bias = lax.dynamic_slice_in_dim(sums_all[3], tensor_rank * head_loc, head_loc, 0)
    g_skip = lax.dynamic_slice_in_dim(sums_all[4], tensor_rank * head_loc, head_loc, 0)
    g_gnorm = lax.dynamic_slice_in_dim(sums_all[5], tensor_rank * inner_loc, inner_loc, 0)
    gain_loc = norm_gain.shape[0]
    place = lax.axis_index("dp") * tensor_count + tensor_rank
    g_gain = lax.dynamic_slice_in_dim(sums_all[6], place * gain_loc, gain_loc, 0)
    return (
        mixed,
        grad_input,
        g_gain,
        g_zx,
        g_bc,
        g_dt,
        g_conv_x,
        sums_all[1],
        g_a_log,
        g_dt_bias,
        g_skip,
        g_gnorm,
        g_out,
    )


def solution(mesh):
    placed = (
        P(("dp", "tensor"), None),
        P("dp", None),
        P(("dp", "tensor")),
        P("dp", None, "tensor"),
        P(("dp", "tensor"), None),
        P("dp", "tensor"),
        P(None, "tensor"),
        P(),
        P("tensor"),
        P("tensor"),
        P("tensor"),
        P("tensor"),
        P("dp", "tensor"),
        P(("dp", "tensor"), None),
    )
    return jax.shard_map(
        body,
        mesh=mesh,
        in_specs=placed,
        out_specs=(
            P(("dp", "tensor"), None),
            P(("dp", "tensor"), None),
            P(("dp", "tensor")),
            P("dp", None, "tensor"),
            P(("dp", "tensor"), None),
            P("dp", "tensor"),
            P(None, "tensor"),
            P(),
            P("tensor"),
            P("tensor"),
            P("tensor"),
            P("tensor"),
            P("dp", "tensor"),
        ),
        check_vma=False,
    )
```

```python
import jax
import jax.numpy as jnp
from jax import lax
from jax.experimental import pallas as pl
from jax.experimental.pallas import tpu as pltpu
from jax.sharding import PartitionSpec as P

BLOCK_LEN = 256


epsilon = 1e-05
exact_mode = lax.Precision.HIGHEST


def causal_conv(values, weights, segments):
    taps = weights.shape[0] - 1
    length = values.shape[0]
    padded = jnp.concatenate([jnp.zeros((taps - 1, values.shape[1]), values.dtype), values], axis=0)
    seg_pad = jnp.concatenate([jnp.full((taps - 1,), -1, jnp.int32), segments])
    summed = jnp.zeros_like(values) + weights[taps]
    for offset in range(taps):
        matched = seg_pad[offset : offset + length] == segments
        summed = summed + weights[offset] * jnp.where(
            matched[:, None], padded[offset : offset + length], 0.0
        )
    return summed


def exact_dot(left, right, dims):
    return lax.dot_general(
        left, right, (dims, ((), ())), precision=exact_mode, preferred_element_type=jnp.float32
    )


def low_dot(left, right, dims):
    return lax.dot_general(
        left.astype(jnp.bfloat16),
        right.astype(jnp.bfloat16),
        (dims, ((), ())),
        preferred_element_type=jnp.float32,
    )


ROWS_COLS = ((1,), (0,))
COLS_COLS = ((1,), (1,))
ROWS_ROWS = ((0,), (0,))


def block_terms(x_ref, bc_ref, cols_ref, rows_ref, rate_row_ref, rate_col_ref):
    heads = rate_row_ref.shape[1]
    span, inner = x_ref.shape
    width = inner // heads
    half = bc_ref.shape[1] // 2
    cols = cols_ref[...]
    rows = rows_ref[...]
    dt = cols[:, :heads]
    start = cols[:, heads + 1 : heads + 2]
    tail = cols[:, heads + 2 : heads + 3]
    row_ids = lax.broadcasted_iota(jnp.int32, (span, span), 0)
    col_ids = lax.broadcasted_iota(jnp.int32, (span, span), 1)
    lower = row_ids >= col_ids
    tri = jnp.where(lower, 1.0, 0.0)
    allowed = lower & (cols[:, heads : heads + 1] == rows[heads : heads + 1, :])
    cum_col = exact_dot(tri, dt * rate_row_ref[...], ROWS_COLS)
    cum_row = exact_dot(rows[:heads, :] * rate_col_ref[...], tri, COLS_COLS)
    total = cum_col[span - 1 : span, :]
    last_start = start[span - 1 : span, :]
    kept = last_start * jnp.exp(total)
    head_ids = lax.broadcasted_iota(jnp.int32, (heads, inner), 0)
    chan_ids = lax.broadcasted_iota(jnp.int32, (heads, inner), 1)
    member = jnp.where(
        (chan_ids >= head_ids * width) & (chan_ids < (head_ids + 1) * width), 1.0, 0.0
    )
    spread = exact_dot(
        jnp.concatenate([dt, start * jnp.exp(cum_col), tail * jnp.exp(total - cum_col)], axis=0),
        member,
        ROWS_COLS,
    )
    kept_wide = jnp.broadcast_to(
        last_start * jnp.exp(cum_row[:, span - 1 : span]), (heads, half)
    )
    kept_state = exact_dot(member, kept_wide, ROWS_ROWS)
    x = x_ref[...]
    dt_wide, start_wide, tail_wide = spread[:span], spread[span : 2 * span], spread[2 * span :]
    in_map = bc_ref[:, :half].astype(jnp.bfloat16)
    out_map = bc_ref[:, half:].astype(jnp.bfloat16)
    inner_prod = low_dot(out_map, in_map, COLS_COLS)

    def decay(head):
        gaps = cum_col[:, head : head + 1] - cum_row[head : head + 1, :]
        return jnp.exp(jnp.where(allowed, gaps, -jnp.inf))

    return (
        heads, width, x, x * dt_wide, dt_wide, start_wide, tail_wide,
        in_map, out_map, inner_prod, decay, kept, kept_state, member, tri,
    )


def forward_kernel(
    x_ref, bc_ref, cols_ref, rows_ref, rate_row_ref, rate_col_ref, skip_ref,
    y_ref, states_ref, state,
):
    @pl.when(pl.program_id(0) == 0)
    def _():
        state[...] = jnp.zeros_like(state)

    (heads, width, x, x_dt, dt_wide, start_wide, tail_wide,
     in_map, out_map, inner_prod, decay, kept, kept_state, member, tri) = block_terms(
        x_ref, bc_ref, cols_ref, rows_ref, rate_row_ref, rate_col_ref
    )
    before = state[...]
    states_ref[0] = before
    x_low = x_dt.astype(jnp.bfloat16)
    local = [
        low_dot(inner_prod * decay(h), x_low[:, h * width : (h + 1) * width], ROWS_COLS)
        for h in range(heads)
    ]
    y = jnp.concatenate(local, axis=1) + start_wide * low_dot(out_map, before, COLS_COLS)
    y_ref[...] = (y + skip_ref[...] * x).astype(y_ref.dtype)
    state[...] = kept_state * before + low_dot(x_dt * tail_wide, in_map, ROWS_ROWS)


def backward_kernel(
    x_ref, bc_ref, cols_ref, rows_ref, rate_row_ref, rate_col_ref, skip_ref, dy_ref, states_ref,
    dx_ref, dbc_ref, ddt_ref, da_ref, dskip_ref, dstate,
):
    @pl.when(pl.program_id(0) == 0)
    def _():
        dstate[...] = jnp.zeros_like(dstate)
        dskip_ref[...] = jnp.zeros_like(dskip_ref)

    (heads, width, x, x_dt, dt_wide, start_wide, tail_wide,
     in_map, out_map, inner_prod, decay, kept, kept_state, member, tri) = block_terms(
        x_ref, bc_ref, cols_ref, rows_ref, rate_row_ref, rate_col_ref
    )
    half = in_map.shape[1]
    before = states_ref[0]
    after_grad = dstate[...]
    dy_low = dy_ref[...]
    dy = dy_low.astype(jnp.float32)
    x_low = x_dt.astype(jnp.bfloat16)
    local, back = [], []
    d_prod = jnp.zeros_like(inner_prod)
    for h in range(heads):
        part = slice(h * width, (h + 1) * width)
        fade = decay(h)
        scores = (inner_prod * fade).astype(jnp.bfloat16)
        local.append(low_dot(scores, x_low[:, part], ROWS_COLS))
        back.append(low_dot(scores, dy_low[:, part], ROWS_ROWS))
        d_prod = d_prod + low_dot(dy_low[:, part], x_low[:, part], COLS_COLS) * fade
    dy_start = (dy * start_wide).astype(jnp.bfloat16)
    x_tail = (x_dt * tail_wide).astype(jnp.bfloat16)
    y = jnp.concatenate(local, axis=1) + start_wide * low_dot(out_map, before, COLS_COLS)
    from_state = tail_wide * low_dot(in_map, after_grad, COLS_COLS)
    local_back = jnp.concatenate(back, axis=1)
    d_xdt = local_back + from_state
    x_exact = x_low.astype(jnp.float32)
    tail_terms = from_state * x_exact
    d_cum_wide = dy * y - local_back * x_exact - tail_terms
    d_both = exact_dot(
        jnp.concatenate([d_cum_wide, d_xdt * x], axis=0), member, COLS_COLS
    )
    span = x.shape[0]
    tail_sum = jnp.sum(tail_terms, axis=0, keepdims=True)
    kept_sum = exact_dot(jnp.ones((8, half), jnp.float32), after_grad * before, COLS_COLS)
    last_both = exact_dot(
        jnp.concatenate([jnp.broadcast_to(tail_sum, kept_sum.shape), kept_sum], axis=0),
        member,
        COLS_COLS,
    )
    d_last = last_both[0:1] + kept * last_both[8:9]
    d_a = exact_dot(tri, d_both[:span], ROWS_ROWS) + d_last
    da_ref[...] = d_a
    ddt_ref[...] = d_both[span:] + d_a * rate_row_ref[...]
    dx_ref[...] = d_xdt * dt_wide + skip_ref[...] * dy
    dskip_ref[...] += jnp.broadcast_to(jnp.sum(dy * x, axis=0, keepdims=True), dskip_ref.shape)
    dbc_ref[:, :half] = low_dot(d_prod, out_map, ROWS_ROWS) + low_dot(
        x_tail, after_grad, ROWS_COLS
    )
    dbc_ref[:, half:] = low_dot(d_prod, in_map, ROWS_COLS) + low_dot(dy_start, before, ROWS_COLS)
    dstate[...] = kept_state * after_grad + low_dot(dy_start, out_map, ROWS_ROWS)


def block_specs(length, inner, maps, lanes, heads, order):
    return [
        pl.BlockSpec((BLOCK_LEN, inner), lambda i: (order(i), 0)),
        pl.BlockSpec((BLOCK_LEN, maps), lambda i: (order(i), 0)),
        pl.BlockSpec((BLOCK_LEN, lanes), lambda i: (order(i), 0)),
        pl.BlockSpec((lanes, BLOCK_LEN), lambda i: (0, order(i))),
        pl.BlockSpec((1, heads), lambda i: (0, 0)),
        pl.BlockSpec((heads, 1), lambda i: (0, 0)),
        pl.BlockSpec((1, inner), lambda i: (0, 0)),
    ]


def limits():
    return pltpu.CompilerParams(vmem_limit_bytes=48 * 1024 * 1024)


def scan_forward(xs, maps, cols, rows, rates, skip_wide):
    length, inner = xs.shape
    heads = rates.shape[0]
    half = maps.shape[1] // 2
    blocks = length // BLOCK_LEN
    return pl.pallas_call(
        forward_kernel,
        grid=(blocks,),
        in_specs=block_specs(length, inner, maps.shape[1], cols.shape[1], heads, lambda i: i),
        out_specs=[
            pl.BlockSpec((BLOCK_LEN, inner), lambda i: (i, 0)),
            pl.BlockSpec((1, inner, half), lambda i: (i, 0, 0)),
        ],
        out_shape=[
            jax.ShapeDtypeStruct((length, inner), jnp.bfloat16),
            jax.ShapeDtypeStruct((blocks, inner, half), jnp.float32),
        ],
        scratch_shapes=[pltpu.VMEM((inner, half), jnp.float32)],
        compiler_params=limits(),
        cost_estimate=pl.CostEstimate(
            flops=12 * 10**9, bytes_accessed=24 * 10**6, transcendentals=10**7
        ),
        name="scan_forward",
    )(xs, maps, cols, rows, rates[None, :], rates[:, None], skip_wide)


def scan_backward(xs, maps, cols, rows, rates, skip_wide, dy, states):
    length, inner = xs.shape
    heads = rates.shape[0]
    half = maps.shape[1] // 2
    blocks = length // BLOCK_LEN
    last = blocks - 1
    return pl.pallas_call(
        backward_kernel,
        grid=(blocks,),
        in_specs=block_specs(
            length, inner, maps.shape[1], cols.shape[1], heads, lambda i: last - i
        )
        + [
            pl.BlockSpec((BLOCK_LEN, inner), lambda i: (last - i, 0)),
            pl.BlockSpec((1, inner, half), lambda i: (last - i, 0, 0)),
        ],
        out_specs=[
            pl.BlockSpec((BLOCK_LEN, inner), lambda i: (last - i, 0)),
            pl.BlockSpec((BLOCK_LEN, 2 * half), lambda i: (last - i, 0)),
            pl.BlockSpec((BLOCK_LEN, heads), lambda i: (last - i, 0)),
            pl.BlockSpec((BLOCK_LEN, heads), lambda i: (last - i, 0)),
            pl.BlockSpec((8, inner), lambda i: (0, 0)),
        ],
        out_shape=[
            jax.ShapeDtypeStruct((length, inner), jnp.float32),
            jax.ShapeDtypeStruct((length, 2 * half), jnp.float32),
            jax.ShapeDtypeStruct((length, heads), jnp.float32),
            jax.ShapeDtypeStruct((length, heads), jnp.float32),
            jax.ShapeDtypeStruct((8, inner), jnp.float32),
        ],
        scratch_shapes=[pltpu.VMEM((inner, half), jnp.float32)],
        compiler_params=limits(),
        cost_estimate=pl.CostEstimate(
            flops=30 * 10**9, bytes_accessed=40 * 10**6, transcendentals=10**7
        ),
        name="scan_backward",
    )(xs, maps, cols, rows, rates[None, :], rates[:, None], skip_wide, dy, states)


def scan_inputs(step, segments):
    length, heads = step.shape
    ends = segments.reshape(-1, BLOCK_LEN)[:, -1]
    before = jnp.concatenate([jnp.full((1,), -1, segments.dtype), ends[:-1]])
    blocked = segments.reshape(-1, BLOCK_LEN)
    start = (blocked == before[:, None]).reshape(-1)
    tail = (blocked == ends[:, None]).reshape(-1)
    marks = jnp.stack([segments, start, tail], axis=0).astype(jnp.float32)
    extra = -(heads + 3) % 8
    rows = jnp.concatenate([step.T, marks, jnp.zeros((extra, length), jnp.float32)], axis=0)
    return rows.T, rows


def conv_parts(inner_x, bc_raw, dt_raw, conv_x, conv_bc, dt_bias, segments):
    xs = jax.nn.silu(causal_conv(inner_x, conv_x, segments))
    maps = jax.nn.silu(causal_conv(bc_raw, conv_bc, segments))
    return xs, maps, jax.nn.softplus(dt_raw + dt_bias)


def contract_rows(left, right):
    return lax.dot_general(
        left, right, (((0,), (0,)), ((), ())), preferred_element_type=jnp.float32
    )


def contract_cols(left, right):
    return lax.dot_general(
        left, right, (((1,), (1,)), ((), ())), preferred_element_type=jnp.float32
    )


def spread_part(part, axis_pos, parts, rank):
    full_shape = list(part.shape)
    full_shape[axis_pos] = part.shape[axis_pos] * parts
    zeros_full = jnp.zeros(tuple(full_shape), jnp.float32)
    return lax.dynamic_update_slice_in_dim(zeros_full, part, rank * part.shape[axis_pos], axis_pos)


def body(
    hidden_in,
    segment_ids,
    norm_gain,
    w_zx,
    w_bc,
    w_dt,
    conv_x,
    conv_bc,
    a_log,
    dt_bias,
    skip_gain,
    gnorm_gain,
    w_out,
    grad_out,
):
    model_dim = hidden_in.shape[1]
    tensor_count = lax.axis_size("tensor")
    tensor_rank = lax.axis_index("tensor")
    rows_loc = w_zx.shape[0]
    inner_loc = w_zx.shape[2]
    heads = w_dt.shape[1]
    maps_dim = w_bc.shape[1]
    inner_total = inner_loc * tensor_count
    hidden_all = lax.all_gather(hidden_in, "tensor", axis=0, tiled=True)
    few = jnp.concatenate([w_bc, jnp.pad(norm_gain[:, None], ((0, 0), (0, 127)))], axis=1)
    few_rows = lax.all_gather(few, "tensor", axis=0, tiled=True)
    w_mine = jnp.concatenate(
        [
            w_zx.reshape(rows_loc, 2 * inner_loc),
            few_rows[:, :maps_dim],
            w_dt,
            few_rows[:, maps_dim : maps_dim + 128 - heads],
        ],
        axis=1,
    )
    hidden_all, w_mine, cot_mine = lax.optimization_barrier((hidden_all, w_mine, grad_out))
    w_all = lax.all_gather(
        jnp.concatenate([w_mine, w_out], axis=1), "dp", axis=0, tiled=True
    )
    w_out_rows = w_all[:, w_mine.shape[1] :]
    w_all = w_all[:, : w_mine.shape[1]]
    cot_all = lax.all_gather(cot_mine, "tensor", axis=0, tiled=True)
    bc_at = 2 * inner_loc
    dt_at = bc_at + maps_dim
    gain_val = w_all[:, dt_at + heads].astype(jnp.float32)
    hidden = hidden_in.astype(jnp.float32)
    pre_scale = lax.rsqrt(jnp.mean(hidden * hidden, -1, keepdims=True) + epsilon)
    hidden_val = hidden_all.astype(jnp.float32)
    scale_all = lax.rsqrt(jnp.mean(hidden_val * hidden_val, -1, keepdims=True) + epsilon)
    normed_all = (hidden_val * scale_all * gain_val).astype(jnp.bfloat16)
    gate_low = jnp.dot(
        normed_all, w_all[:, :inner_loc], preferred_element_type=jnp.float32
    ).astype(jnp.bfloat16)
    inner_x = jnp.dot(
        normed_all, w_all[:, inner_loc:bc_at], preferred_element_type=jnp.float32
    )
    few_proj = jnp.dot(normed_all, w_all[:, bc_at:], preferred_element_type=jnp.float32)
    bc_raw = few_proj[:, :maps_dim]
    dt_raw = few_proj[:, maps_dim : maps_dim + heads]
    segments = segment_ids[0]

    def local_conv(inner_in, bc_in, dt_in, conv_xin, conv_bcin, dt_biasin):
        return conv_parts(inner_in, bc_in, dt_in, conv_xin, conv_bcin, dt_biasin, segments)

    (xs, maps, step), conv_back = jax.vjp(
        local_conv, inner_x, bc_raw, dt_raw, conv_x, conv_bc, dt_bias
    )
    rates = -jnp.exp(a_log)
    width = inner_loc // heads
    skip_wide = jnp.repeat(skip_gain, width)[None, :]
    cols, rows = scan_inputs(step, segments)
    y_low, states = scan_forward(xs, maps, cols, rows, rates, skip_wide)
    y_val = y_low.astype(jnp.float32)
    z_val = gate_low.astype(jnp.float32)
    sigma_z = jax.nn.sigmoid(z_val)
    gated = y_val * z_val * sigma_z
    gn_gain = gnorm_gain.astype(jnp.float32)
    d_gate_norm = jnp.dot(cot_all, w_out_rows, preferred_element_type=jnp.float32)
    scaled_grad = d_gate_norm * gn_gain
    token_sums = lax.psum(
        jnp.stack([jnp.sum(gated * gated, -1), jnp.sum(scaled_grad * gated, -1)]), "tensor"
    )
    gate_scale = lax.rsqrt(token_sums[0] / inner_total + epsilon)[:, None]
    cross_sum = token_sums[1]
    d_gated = gate_scale * scaled_grad - gated * gate_scale**3 * (cross_sum / inner_total)[:, None]
    dy_low = (d_gated * z_val * sigma_z).astype(jnp.bfloat16)
    dz_low = (d_gated * y_val * sigma_z * (1.0 + z_val * (1.0 - sigma_z))).astype(jnp.bfloat16)
    normed_gate = (gated * gate_scale * gn_gain).astype(jnp.bfloat16)
    d_gain_part = jnp.sum(d_gate_norm * gated * gate_scale, 0)
    branch_part = contract_cols(normed_gate, w_out_rows).astype(jnp.bfloat16)
    d_w_early = jnp.concatenate(
        [
            contract_rows(cot_all, normed_gate).astype(jnp.bfloat16),
            contract_rows(normed_all, dz_low).astype(jnp.bfloat16),
        ],
        axis=1,
    )
    dy_low, branch_part, d_w_early = lax.optimization_barrier((dy_low, branch_part, d_w_early))
    branch = lax.psum_scatter(branch_part, "tensor", scatter_dimension=0, tiled=True)
    g_early = lax.psum_scatter(d_w_early, "dp", scatter_dimension=0, tiled=True)
    dxs, dmaps, dstep, d_rate_terms, dskip_rows = scan_backward(
        xs, maps, cols, rows, rates, skip_wide, dy_low, states
    )
    d_a_log = jnp.sum(d_rate_terms * step, 0) * rates
    d_skip = jnp.sum(dskip_rows[0].reshape(heads, width), 1)
    d_inner, d_bc, d_dt, d_conv_x, d_conv_bc, d_dt_bias = conv_back((dxs, dmaps, dstep))
    d_rest = jnp.concatenate(
        [
            d_inner.astype(jnp.bfloat16),
            d_bc.astype(jnp.bfloat16),
            d_dt.astype(jnp.bfloat16),
            jnp.zeros((d_dt.shape[0], 128 - heads), jnp.bfloat16),
        ],
        axis=1,
    )
    term = (
        contract_cols(dz_low, w_all[:, :inner_loc]) + contract_cols(d_rest, w_all[:, inner_loc:])
    ).astype(jnp.bfloat16)
    term, branch, g_early, d_rest = lax.optimization_barrier((term, branch, g_early, d_rest))
    mixed = (hidden + branch.astype(jnp.float32)).astype(jnp.bfloat16)
    g_out = g_early[:, :inner_loc].astype(jnp.float32)
    d_normed = lax.psum_scatter(term, "tensor", scatter_dimension=0, tiled=True).astype(
        jnp.float32
    )
    d_w = contract_rows(normed_all, d_rest).astype(jnp.bfloat16)
    g_rest = lax.psum_scatter(d_w, "dp", scatter_dimension=0, tiled=True)
    g_bc = lax.psum_scatter(
        g_rest[:, inner_loc : inner_loc + maps_dim], "tensor", scatter_dimension=0, tiled=True
    ).astype(jnp.float32)
    g_zx = (
        jnp.stack([g_early[:, inner_loc:], g_rest[:, :inner_loc]], axis=1).astype(jnp.float32)
    )
    g_dt = g_rest[:, inner_loc + maps_dim : inner_loc + maps_dim + heads].astype(jnp.float32)
    pre_grad = d_normed * gain_val
    d_hidden = pre_scale * pre_grad - hidden * pre_scale**3 * jnp.mean(
        pre_grad * hidden, -1, keepdims=True
    )
    grad_input = grad_out.astype(jnp.float32) + d_hidden
    d_norm_gain = jnp.sum(term.astype(jnp.float32) * hidden_val * scale_all, 0)
    sums_all = lax.psum(
        (
            spread_part(d_conv_x, 1, tensor_count, tensor_rank),
            d_conv_bc,
            spread_part(d_a_log, 0, tensor_count, tensor_rank),
            spread_part(d_dt_bias, 0, tensor_count, tensor_rank),
            spread_part(d_skip, 0, tensor_count, tensor_rank),
            spread_part(d_gain_part, 0, tensor_count, tensor_rank),
            d_norm_gain,
        ),
        ("dp", "tensor"),
    )
    head_loc = d_a_log.shape[0]
    g_conv_x = lax.dynamic_slice_in_dim(sums_all[0], tensor_rank * inner_loc, inner_loc, 1)
    g_a_log = lax.dynamic_slice_in_dim(sums_all[2], tensor_rank * head_loc, head_loc, 0)
    g_dt_bias = lax.dynamic_slice_in_dim(sums_all[3], tensor_rank * head_loc, head_loc, 0)
    g_skip = lax.dynamic_slice_in_dim(sums_all[4], tensor_rank * head_loc, head_loc, 0)
    g_gnorm = lax.dynamic_slice_in_dim(sums_all[5], tensor_rank * inner_loc, inner_loc, 0)
    gain_loc = norm_gain.shape[0]
    place = lax.axis_index("dp") * tensor_count + tensor_rank
    g_gain = lax.dynamic_slice_in_dim(sums_all[6], place * gain_loc, gain_loc, 0)
    return (
        mixed,
        grad_input,
        g_gain,
        g_zx,
        g_bc,
        g_dt,
        g_conv_x,
        sums_all[1],
        g_a_log,
        g_dt_bias,
        g_skip,
        g_gnorm,
        g_out,
    )


def solution(mesh):
    placed = (
        P(("dp", "tensor"), None),
        P("dp", None),
        P(("dp", "tensor")),
        P("dp", None, "tensor"),
        P(("dp", "tensor"), None),
        P("dp", "tensor"),
        P(None, "tensor"),
        P(),
        P("tensor"),
        P("tensor"),
        P("tensor"),
        P("tensor"),
        P("dp", "tensor"),
        P(("dp", "tensor"), None),
    )
    return jax.shard_map(
        body,
        mesh=mesh,
        in_specs=placed,
        out_specs=(
            P(("dp", "tensor"), None),
            P(("dp", "tensor"), None),
            P(("dp", "tensor")),
            P("dp", None, "tensor"),
            P(("dp", "tensor"), None),
            P("dp", "tensor"),
            P(None, "tensor"),
            P(),
            P("tensor"),
            P("tensor"),
            P("tensor"),
            P("tensor"),
            P("dp", "tensor"),
        ),
        check_vma=False,
    )
```
